32 devices in a mesh: seq: 8 (over z, core), tp: 4 (over y, x).
Axes of the slice: x: 2, y: 2, z: 4, core: 2. Of those that a mesh axis runs over, the one named last changes fastest.
Arguments:
- features: bfloat16 [3, 2048, 8192], P(None, 'seq', 'tp'), may hold values from -6 to 6
- short_filter: float32 [7, 3, 8192], P(None, None, 'tp'), may hold values from -2 to 2
- medium_filter: float32 [128, 8192], P('seq', 'tp'), may hold values from -0.5 to 0.5
- skip_gain: float32 [8192], P('tp'), may hold values from -4 to 4
- out_weight: bfloat16 [8192, 8192], P(None, 'tp'), may hold values from -0.0625 to 0.0625
Outputs:
- block_out: bfloat16 [2048, 8192], P('seq', 'tp')
The draws below stay inside these ranges and needn't reach their ends.
All inputs are finite; a program needn't handle non-finite values.
Results may differ from the reference program's by a relative error of at most 0.0058.
Values may be sent and summed in bfloat16 or wider, within the bound.
A program may use at most 128 MiB of HBM per device.

```python
import math
import jax
import jax.numpy as jnp
from jax import lax

D = 8192
TAPS = 128
SHORT = 7
TOKENS = 2048


def block_levels(key, extent, cuts, smallest, high):
    def one(axis_at, shards_of):
        heights = jax.random.uniform(jax.random.fold_in(jax.random.fold_in(key, 6), axis_at), (shards_of,), jnp.float32, smallest / len(cuts), high / len(cuts))
        return jnp.repeat(jnp.exp(heights), extent[axis_at] // shards_of).reshape((-1,) + (1,) * (len(extent) - axis_at - 1))

    factor_of = one(*cuts[0])
    for cut in cuts[1:]:
        factor_of = factor_of * one(*cut)
    return factor_of


def centred(key, extent, spread, limit, cuts=(), kind=jnp.bfloat16):
    entries = spread * jax.random.normal(key, extent, jnp.float32)
    if cuts:
        entries = entries * block_levels(key, extent, cuts, -0.22, 0.18)
    return jnp.clip(entries, -limit, limit).astype(kind)


def setup_inputs(seed: int = 0) -> dict:
    seeds = jax.random.split(jax.random.key(seed), 6)
    features = centred(seeds[0], (3, TOKENS, D), 1.0, 6.0, ((1, 8), (2, 4)))
    short_filter = centred(seeds[1], (SHORT, 3, D), SHORT ** -0.5, 2.0, ((2, 4),), jnp.float32)
    medium_filter = centred(seeds[2], (TAPS, D), TAPS ** -0.5, 0.5, ((0, 8), (1, 4)), jnp.float32)
    skip_gain = centred(seeds[3], (D,), 1.0, 4.0, ((0, 4),), jnp.float32)
    out_weight = centred(seeds[4], (D, D), D ** -0.5, 0.0625, ((1, 4),))
    return {"features": features, "short_filter": short_filter, "medium_filter": medium_filter, "skip_gain": skip_gain, "out_weight": out_weight}


def causal(values, kernel):
    reach = kernel.shape[0]
    length = values.shape[0]
    padded = jnp.pad(values, ((reach - 1, 0), (0, 0)))

    def add_tap(index, total):
        begin = (jnp.int32(reach - 1) - index).astype(jnp.int32)
        window = lax.dynamic_slice_in_dim(padded, begin, length, 0)
        return total + kernel[index] * window

    return lax.fori_loop(jnp.int32(0), jnp.int32(reach), add_tap, jnp.zeros_like(values))


def gate_block(pieces):
    feature_block, short_block, medium_block, skip_block = pieces
    widened = feature_block.astype(jnp.float32)
    query_conv = causal(widened[0], short_block[:, 0, :])
    key_conv = causal(widened[1], short_block[:, 1, :])
    value_conv = causal(widened[2], short_block[:, 2, :])
    product = (key_conv * value_conv).astype(jnp.bfloat16)
    product_wide = product.astype(jnp.float32)
    longer = causal(product_wide, medium_block)
    return (query_conv * (longer + skip_block * product_wide)).astype(jnp.bfloat16)


def reference(features, short_filter, medium_filter, skip_gain, out_weight):
    width = features.shape[2]
    length = features.shape[1]
    block_width = math.gcd(width, 512)
    blocks = width // block_width
    feature_blocks = features.reshape(3, length, blocks, block_width).transpose(2, 0, 1, 3)
    short_blocks = short_filter.reshape(short_filter.shape[0], 3, blocks, block_width).transpose(2, 0, 1, 3)
    medium_blocks = medium_filter.reshape(medium_filter.shape[0], blocks, block_width).transpose(1, 0, 2)
    skip_blocks = skip_gain.reshape(blocks, block_width)
    gated_blocks = lax.map(gate_block, (feature_blocks, short_blocks, medium_blocks, skip_blocks))
    gated_rows = gated_blocks.transpose(1, 0, 2).reshape(length, width)
    return jnp.dot(gated_rows, out_weight, preferred_element_type=jnp.float32).astype(jnp.bfloat16)
```

```python
import functools

import jax
import jax.numpy as jnp
import ml_dtypes
import numpy as np
from jax import lax
from jax.experimental import pallas as pl
from jax.experimental.pallas import tpu as pltpu
from jax.sharding import PartitionSpec as P

MESH = pl.DeviceIdType.MESH
F32 = jnp.float32
BF16 = jnp.bfloat16


def passed_along(value, axis, steps):
    count = lax.axis_size(axis)
    leading, last = (max(0, -steps), min(count, count - steps))
    return lax.ppermute(value, axis, [(source, source + steps) for source in range(leading, last)])


def depthwise(extended, kernel):
    channels = extended.shape[1]
    return lax.conv_general_dilated(
        extended[None],
        kernel[::-1][:, None, :],
        (1,),
        "VALID",
        dimension_numbers=("NWC", "WIO", "NWC"),
        feature_group_count=channels,
        precision=lax.Precision.HIGHEST,
    )[0]


def on_device(features, short_filter, medium_filter, skip_gain, out_weight):
    taps_full = lax.all_gather(medium_filter, "seq", axis=0, tiled=True)
    long_reach = taps_full.shape[0]
    short_reach = short_filter.shape[0]
    tok_rows = features.shape[1]
    lead_rows = passed_along(features[:, tok_rows - (short_reach - 1) :, :], "seq", 1)
    extended = jnp.concatenate([lead_rows, features], 1).astype(F32)
    query_conv = depthwise(extended[0], short_filter[:, 0, :])
    key_conv = depthwise(extended[1], short_filter[:, 1, :])
    value_conv = depthwise(extended[2], short_filter[:, 2, :])
    product = (key_conv * value_conv).astype(BF16)
    lead_product = passed_along(product[tok_rows - (long_reach - 1) :], "seq", 1)
    product_ext = jnp.concatenate([lead_product, product], 0)
    longer = depthwise(product_ext.astype(F32), taps_full)
    gated_rows = (query_conv * (longer + skip_gain * product.astype(F32))).astype(BF16)
    gathered = lax.all_gather(gated_rows, "tp", axis=1, tiled=True)
    result = jnp.dot(gathered, out_weight, preferred_element_type=F32)
    return result.astype(BF16)


def split(matrix):
    high = matrix.astype(ml_dtypes.bfloat16)
    low = (matrix - high.astype(np.float64)).astype(ml_dtypes.bfloat16)
    return np.stack([high, low])


def transforms(points):
    half = points // 2
    at = np.arange(points)
    angle = 2 * np.pi * ((np.arange(half)[:, None] * at[None, :]) % points) / points
    real, imag = np.cos(angle), -np.sin(angle)
    imag[0] = np.where(at % 2 == 0, 1.0, -1.0)
    forward = np.concatenate([real, imag], 0)
    weight = np.full((points, 1), 2.0 / points)
    weight[0] = weight[half] = 1.0 / points
    inverse = (forward * weight).T[half:]
    return split(forward), split(inverse)


def dot(a, b):
    return jnp.dot(a, b, preferred_element_type=F32)


def kernel(
    sizes,
    features,
    short_ref,
    medium_ref,
    skip_ref,
    forward_ref,
    inverse_ref,
    weight,
    out_ref,
    feat,
    fhalo,
    ext,
    query,
    prod,
    phalo,
    taps,
    gath,
    wbuf,
    acc,
    feat_sem,
    w_sem,
    fh_send,
    fh_recv,
    ph_send,
    ph_recv,
    tap_send,
    tap_recv,
    g_send,
    g_recv,
    d_send,
    d_recv,
):
    seqs, tps, chunks, width, rows, channels, own_taps, short = sizes
    half = rows // 2
    edge = 16
    s = lax.axis_index("seq")
    p = lax.axis_index("tp")
    beside = (p + 1 - 2 * lax.rem(p, 2), lax.rem(p + 2, 4))
    across = 3 - p

    def feat_copy(c):
        return pltpu.make_async_copy(
            features.at[:, :, pl.ds(pl.multiple_of(c * width, width), width)],
            feat.at[c],
            feat_sem.at[c],
        )

    def w_copy(q, c):
        first = pl.multiple_of(q * channels + c * width, width)
        return pltpu.make_async_copy(
            weight.at[pl.ds(first, width), :], wbuf.at[q, c], w_sem.at[q, c]
        )

    def fh_copy(c):
        return pltpu.make_async_remote_copy(
            src_ref=feat.at[c, :, pl.ds(rows - edge, edge), :],
            dst_ref=fhalo.at[c],
            send_sem=fh_send.at[c],
            recv_sem=fh_recv.at[c],
            device_id=(s + 1, p),
            device_id_type=MESH,
        )

    def ph_copy(c):
        return pltpu.make_async_remote_copy(
            src_ref=prod.at[c, pl.ds(half, half), :],
            dst_ref=phalo.at[c],
            send_sem=ph_send.at[c],
            recv_sem=ph_recv.at[c],
            device_id=(s + 1, p),
            device_id_type=MESH,
        )

    def tap_copy(c, k):
        mine = pl.ds(pl.multiple_of(s * own_taps, own_taps), own_taps)
        return pltpu.make_async_remote_copy(
            src_ref=taps.at[c, mine, :],
            dst_ref=taps.at[c, mine, :],
            send_sem=tap_send.at[c, k - 1],
            recv_sem=tap_recv.at[c, k - 1],
            device_id=(lax.rem(s + k, seqs), p),
            device_id_type=MESH,
        )

    def tap_arrival(c, k):
        other = lax.rem(s + seqs - k, seqs)
        theirs = pl.ds(pl.multiple_of(other * own_taps, own_taps), own_taps)
        return pltpu.make_async_remote_copy(
            src_ref=taps.at[c, theirs, :],
            dst_ref=taps.at[c, theirs, :],
            send_sem=tap_send.at[c, k - 1],
            recv_sem=tap_recv.at[c, k - 1],
            device_id=(other, p),
            device_id_type=MESH,
        )

    def g_copy(owner, c, way):
        return pltpu.make_async_remote_copy(
            src_ref=gath.at[owner, c],
            dst_ref=gath.at[owner, c],
            send_sem=g_send.at[c, way],
            recv_sem=g_recv.at[c, way],
            device_id=(s, beside[way]),
            device_id_type=MESH,
        )

    def d_copy(owner, c, way):
        piece = pl.ds(way * half, half)
        return pltpu.make_async_remote_copy(
            src_ref=gath.at[owner, c, piece, :],
            dst_ref=gath.at[owner, c, piece, :],
            send_sem=d_send.at[c, way],
            recv_sem=d_recv.at[c, way],
            device_id=(s, beside[1 - way]),
            device_id_type=MESH,
        )

    for c in range(chunks):
        feat_copy(c).start()
    barrier = pltpu.get_barrier_semaphore()
    for k in range(1, seqs):
        pl.semaphore_signal(
            barrier, inc=1, device_id=(lax.rem(s + k, seqs), p), device_id_type=MESH
        )
    for way in range(2):
        pl.semaphore_signal(barrier, inc=1, device_id=(s, beside[way]), device_id_type=MESH)

    own = pl.ds(pl.multiple_of(s * own_taps, own_taps), own_taps)
    for c in range(chunks):
        taps[c, own, :] = medium_ref[:, c * width : (c + 1) * width].astype(BF16)

    @pl.when(s == 0)
    def _():
        fhalo[...] = jnp.zeros_like(fhalo)
        phalo[...] = jnp.zeros_like(phalo)

    acc[...] = jnp.zeros_like(acc)
    pl.semaphore_wait(barrier, seqs + 1)

    @pl.loop(0, chunks)
    def _(c):
        feat_copy(c).wait()

        @pl.when(s < seqs - 1)
        def _():
            fh_copy(c).start()

        for k in range(1, seqs):
            tap_copy(c, k).start()

    @pl.loop(0, chunks)
    def _(c):
        for q in range(tps):
            w_copy(q, c).start()

    def short_conv(c, stream):
        lanes = pl.ds(pl.multiple_of(c * width, width), width)
        ext[stream, 0:8, :] = fhalo[c, stream, :, :].astype(F32)[edge - 8 :]
        ext[stream, 8:, :] = feat[c, stream, :, :].astype(F32)
        total = None
        for j in range(short):
            term = short_ref[j, pl.ds(stream, 1), lanes] * ext[stream, pl.ds(8 - j, rows), :]
            total = term if total is None else total + term
        return total

    def products(c):
        @pl.when(s > 0)
        def _():
            fh_copy(c).wait_recv()

        prod[c] = (short_conv(c, 1) * short_conv(c, 2)).astype(BF16)

        @pl.when(s < seqs - 1)
        def _():
            ph_copy(c).start()

        query[lax.rem(c, 2)] = short_conv(c, 0)

    def gate(c):
        lanes = pl.ds(pl.multiple_of(c * width, width), width)
        for k in range(1, seqs):
            tap_arrival(c, k).wait_recv()
        f_high, f_low = forward_ref[0], forward_ref[1]
        i_high, i_low = inverse_ref[0], inverse_ref[1]
        h = taps[c]
        spectrum = dot(f_high[:, :half], h) + dot(f_low[:, :half], h)
        skip = skip_ref[pl.ds(0, 1), lanes]
        first = lax.broadcasted_iota(jnp.int32, (half, width), 0) == 0
        h_real = spectrum[:half] + skip
        h_imag = jnp.where(first, 0.0, spectrum[half:])
        h_last = jnp.where(first, spectrum[half:] + skip, h_real)

        def block(before, now):
            window = jnp.concatenate([before, now], 0)
            x = dot(f_high, window) + dot(f_low, window)
            a, b = x[:half], x[half:]
            y = jnp.concatenate([a * h_real - b * h_imag, a * h_imag + b * h_last], 0)
            y_high = y.astype(BF16)
            y_low = (y - y_high.astype(F32)).astype(BF16)
            return dot(i_high, y_high) + dot(i_low, y_high) + dot(i_high, y_low)

        slot = lax.rem(c, 2)
        upper = block(prod[c, 0:half, :], prod[c, half:, :])
        gath[p, c, pl.ds(half, half), :] = (query[slot, pl.ds(half, half), :] * upper).astype(BF16)

        @pl.when(s > 0)
        def _():
            ph_copy(c).wait_recv()

        lower = block(phalo[c], prod[c, 0:half, :])
        gath[p, c, pl.ds(0, half), :] = (query[slot, pl.ds(0, half), :] * lower).astype(BF16)
        for way in range(2):
            g_copy(p, c, way).start()

    def pass_on(c):
        for way in range(2):
            g_copy(beside[way], c, way).wait_recv()
            d_copy(beside[way], c, way).start()

    tile = 512

    def project(c):
        for way in range(2):
            d_copy(across, c, way).wait_recv()
        for q in range(tps):
            w_copy(q, c).wait()

        @pl.loop(0, channels // tile)
        def _(n):
            lanes = pl.ds(pl.multiple_of(n * tile, tile), tile)
            total = acc[:, lanes]
            for q in range(tps):
                total = total + dot(gath[q, c], wbuf[q, c, :, lanes])
            acc[:, lanes] = total

    lag = 3

    @pl.loop(0, chunks + lag)
    def _(i):
        @pl.when(i < chunks)
        def _():
            products(i)

        @pl.when((i >= 1) & (i < chunks + 1))
        def _():
            gate(i - 1)

        @pl.when((i >= 2) & (i < chunks + 2))
        def _():
            pass_on(i - 2)

        @pl.when(i >= lag)
        def _():
            project(i - lag)

    out_ref[...] = acc[...].astype(BF16)

    @pl.loop(0, chunks)
    def _(c):
        @pl.when(s < seqs - 1)
        def _():
            fh_copy(c).wait_send()
            ph_copy(c).wait_send()

        for k in range(1, seqs):
            tap_copy(c, k).wait_send()
        for way in range(2):
            g_copy(p, c, way).wait_send()
            d_copy(beside[way], c, way).wait_send()


def fused(seqs, tps, features, short_filter, medium_filter, skip_gain, out_weight):
    _, rows, channels = features.shape
    own_taps = medium_filter.shape[0]
    short = short_filter.shape[0]
    width = 256
    chunks = channels // width
    edge = 16
    forward, inverse = transforms(rows)
    sizes = (seqs, tps, chunks, width, rows, channels, own_taps, short)
    vmem = pl.BlockSpec(memory_space=pltpu.VMEM)
    anywhere = pl.BlockSpec(memory_space=pl.ANY)
    dma = pltpu.SemaphoreType.DMA
    columns = out_weight.shape[1]
    return pl.pallas_call(
        functools.partial(kernel, sizes),
        out_shape=jax.ShapeDtypeStruct((rows, columns), BF16),
        in_specs=[anywhere, vmem, vmem, vmem, vmem, vmem, anywhere],
        out_specs=vmem,
        scratch_shapes=[
            pltpu.VMEM((chunks, 3, rows, width), BF16),
            pltpu.VMEM((chunks, 3, edge, width), BF16),
            pltpu.VMEM((3, rows + 8, width), F32),
            pltpu.VMEM((2, rows, width), F32),
            pltpu.VMEM((chunks, rows, width), BF16),
            pltpu.VMEM((chunks, rows // 2, width), BF16),
            pltpu.VMEM((chunks, seqs * own_taps, width), BF16),
            pltpu.VMEM((tps, chunks, rows, width), BF16),
            pltpu.VMEM((tps, chunks, width, columns), BF16),
            pltpu.VMEM((rows, columns), F32),
            dma((chunks,)),
            dma((tps, chunks)),
            dma((chunks,)),
            dma((chunks,)),
            dma((chunks,)),
            dma((chunks,)),
            dma((chunks, seqs - 1)),
            dma((chunks, seqs - 1)),
            dma((chunks, 2)),
            dma((chunks, 2)),
            dma((chunks, 2)),
            dma((chunks, 2)),
        ],
        compiler_params=pltpu.CompilerParams(
            collective_id=0, has_side_effects=True, vmem_limit_bytes=56 * 1024 * 1024
        ),
    )(
        features,
        short_filter,
        medium_filter,
        skip_gain.reshape(1, channels),
        jnp.asarray(forward),
        jnp.asarray(inverse),
        out_weight,
    )


def solution(mesh):
    in_specs = (P(None, "seq", "tp"), P(None, None, "tp"), P("seq", "tp"), P("tp"), P(None, "tp"))
    out_specs = P("seq", "tp")
    seqs, tps = mesh.shape["seq"], mesh.shape["tp"]

    def body(features, short_filter, medium_filter, skip_gain, out_weight):
        taps_all = seqs * medium_filter.shape[0]
        fits = (
            tps == 4
            and seqs > 1
            and medium_filter.shape[0] % 16 == 0
            and features.shape[1] == 2 * taps_all
            and features.shape[2] % 512 == 0
            and short_filter.shape[0] <= 9
        )
        if fits:
            return fused(
                seqs, tps, features, short_filter, medium_filter, skip_gain, out_weight
            )
        return on_device(features, short_filter, medium_filter, skip_gain, out_weight)

    return jax.shard_map(body, mesh=mesh, in_specs=in_specs, out_specs=out_specs, check_vma=False)
```

```python
import functools

import jax
import jax.numpy as jnp
import ml_dtypes
import numpy as np
from jax import lax
from jax.experimental import pallas as pl
from jax.experimental.pallas import tpu as pltpu
from jax.sharding import PartitionSpec as P

MESH = pl.DeviceIdType.MESH
F32 = jnp.float32
BF16 = jnp.bfloat16


def passed_along(value, axis, steps):
    count = lax.axis_size(axis)
    leading, last = (max(0, -steps), min(count, count - steps))
    return lax.ppermute(value, axis, [(source, source + steps) for source in range(leading, last)])


def depthwise(extended, kernel):
    channels = extended.shape[1]
    return lax.conv_general_dilated(
        extended[None],
        kernel[::-1][:, None, :],
        (1,),
        "VALID",
        dimension_numbers=("NWC", "WIO", "NWC"),
        feature_group_count=channels,
        precision=lax.Precision.HIGHEST,
    )[0]


def on_device(features, short_filter, medium_filter, skip_gain, out_weight):
    taps_full = lax.all_gather(medium_filter, "seq", axis=0, tiled=True)
    long_reach = taps_full.shape[0]
    short_reach = short_filter.shape[0]
    tok_rows = features.shape[1]
    lead_rows = passed_along(features[:, tok_rows - (short_reach - 1) :, :], "seq", 1)
    extended = jnp.concatenate([lead_rows, features], 1).astype(F32)
    query_conv = depthwise(extended[0], short_filter[:, 0, :])
    key_conv = depthwise(extended[1], short_filter[:, 1, :])
    value_conv = depthwise(extended[2], short_filter[:, 2, :])
    product = (key_conv * value_conv).astype(BF16)
    lead_product = passed_along(product[tok_rows - (long_reach - 1) :], "seq", 1)
    product_ext = jnp.concatenate([lead_product, product], 0)
    longer = depthwise(product_ext.astype(F32), taps_full)
    gated_rows = (query_conv * (longer + skip_gain * product.astype(F32))).astype(BF16)
    gathered = lax.all_gather(gated_rows, "tp", axis=1, tiled=True)
    result = jnp.dot(gathered, out_weight, preferred_element_type=F32)
    return result.astype(BF16)


def split(matrix):
    high = matrix.astype(ml_dtypes.bfloat16)
    low = (matrix - high.astype(np.float64)).astype(ml_dtypes.bfloat16)
    return np.stack([high, low])


def transforms(points):
    half = points // 2
    at = np.arange(points)
    angle = 2 * np.pi * ((np.arange(half)[:, None] * at[None, :]) % points) / points
    real, imag = np.cos(angle), -np.sin(angle)
    imag[0] = np.where(at % 2 == 0, 1.0, -1.0)
    forward = np.concatenate([real, imag], 0)
    weight = np.full((points, 1), 2.0 / points)
    weight[0] = weight[half] = 1.0 / points
    inverse = (forward * weight).T[half:]
    return split(forward), split(inverse)


def dot(a, b):
    return jnp.dot(a, b, preferred_element_type=F32)


def kernel(
    sizes,
    features,
    short_ref,
    medium_ref,
    skip_ref,
    forward_ref,
    inverse_ref,
    weight,
    out_ref,
    feat,
    fhalo,
    ext,
    query,
    prod,
    phalo,
    taps,
    gath,
    wbuf,
    acc,
    feat_sem,
    w_sem,
    fh_send,
    fh_recv,
    ph_send,
    ph_recv,
    tap_send,
    tap_recv,
    g_send,
    g_recv,
    d_send,
    d_recv,
):
    seqs, tps, chunks, width, rows, channels, own_taps, short = sizes
    half = rows // 2
    edge = 16
    s = lax.axis_index("seq")
    p = lax.axis_index("tp")
    beside = (p + 1 - 2 * lax.rem(p, 2), lax.rem(p + 2, 4))
    across = 3 - p

    def feat_copy(c):
        return pltpu.make_async_copy(
            features.at[:, :, pl.ds(pl.multiple_of(c * width, width), width)],
            feat.at[c],
            feat_sem.at[c],
        )

    def w_copy(q, c):
        first = pl.multiple_of(q * channels + c * width, width)
        return pltpu.make_async_copy(
            weight.at[pl.ds(first, width), :], wbuf.at[q, c], w_sem.at[q, c]
        )

    def fh_copy(c):
        return pltpu.make_async_remote_copy(
            src_ref=feat.at[c, :, pl.ds(rows - edge, edge), :],
            dst_ref=fhalo.at[c],
            send_sem=fh_send.at[c],
            recv_sem=fh_recv.at[c],
            device_id=(s + 1, p),
            device_id_type=MESH,
        )

    def ph_copy(c):
        return pltpu.make_async_remote_copy(
            src_ref=prod.at[c, pl.ds(half, half), :],
            dst_ref=phalo.at[c],
            send_sem=ph_send.at[c],
            recv_sem=ph_recv.at[c],
            device_id=(s + 1, p),
            device_id_type=MESH,
        )

    def tap_copy(c, k):
        mine = pl.ds(pl.multiple_of(s * own_taps, own_taps), own_taps)
        return pltpu.make_async_remote_copy(
            src_ref=taps.at[c, mine, :],
            dst_ref=taps.at[c, mine, :],
            send_sem=tap_send.at[c, k - 1],
            recv_sem=tap_recv.at[c, k - 1],
            device_id=(lax.rem(s + k, seqs), p),
            device_id_type=MESH,
        )

    def tap_arrival(c, k):
        other = lax.rem(s + seqs - k, seqs)
        theirs = pl.ds(pl.multiple_of(other * own_taps, own_taps), own_taps)
        return pltpu.make_async_remote_copy(
            src_ref=taps.at[c, theirs, :],
            dst_ref=taps.at[c, theirs, :],
            send_sem=tap_send.at[c, k - 1],
            recv_sem=tap_recv.at[c, k - 1],
            device_id=(other, p),
            device_id_type=MESH,
        )

    def g_copy(owner, c, way):
        return pltpu.make_async_remote_copy(
            src_ref=gath.at[owner, c],
            dst_ref=gath.at[owner, c],
            send_sem=g_send.at[c, way],
            recv_sem=g_recv.at[c, way],
            device_id=(s, beside[way]),
            device_id_type=MESH,
        )

    def d_copy(owner, c, way):
        piece = pl.ds(way * half, half)
        return pltpu.make_async_remote_copy(
            src_ref=gath.at[owner, c, piece, :],
            dst_ref=gath.at[owner, c, piece, :],
            send_sem=d_send.at[c, way],
            recv_sem=d_recv.at[c, way],
            device_id=(s, beside[1 - way]),
            device_id_type=MESH,
        )

    for c in range(chunks):
        feat_copy(c).start()
    barrier = pltpu.get_barrier_semaphore()
    for k in range(1, seqs):
        pl.semaphore_signal(
            barrier, inc=1, device_id=(lax.rem(s + k, seqs), p), device_id_type=MESH
        )
    for way in range(2):
        pl.semaphore_signal(barrier, inc=1, device_id=(s, beside[way]), device_id_type=MESH)

    own = pl.ds(pl.multiple_of(s * own_taps, own_taps), own_taps)
    for c in range(chunks):
        taps[c, own, :] = medium_ref[:, c * width : (c + 1) * width].astype(BF16)

    @pl.when(s == 0)
    def _():
        fhalo[...] = jnp.zeros_like(fhalo)
        phalo[...] = jnp.zeros_like(phalo)

    acc[...] = jnp.zeros_like(acc)
    pl.semaphore_wait(barrier, seqs + 1)

    def share(c):
        feat_copy(c).wait()

        @pl.when(s < seqs - 1)
        def _():
            fh_copy(c).start()

        for k in range(1, seqs):
            tap_copy(c, k).start()

    ahead = 2

    @pl.loop(0, min(ahead, chunks))
    def _(c):
        share(c)

    @pl.loop(0, chunks)
    def _(c):
        for q in range(tps):
            w_copy(q, c).start()

    def short_conv(c, stream):
        lanes = pl.ds(pl.multiple_of(c * width, width), width)
        ext[stream, 0:8, :] = fhalo[c, stream, :, :].astype(F32)[edge - 8 :]
        ext[stream, 8:, :] = feat[c, stream, :, :].astype(F32)
        total = None
        for j in range(short):
            term = short_ref[stream, pl.ds(j, 1), lanes] * ext[stream, pl.ds(8 - j, rows), :]
            total = term if total is None else total + term
        return total

    def products(c):
        @pl.when(s > 0)
        def _():
            fh_copy(c).wait_recv()

        prod[c] = (short_conv(c, 1) * short_conv(c, 2)).astype(BF16)

        @pl.when(s < seqs - 1)
        def _():
            ph_copy(c).start()

        query[lax.rem(c, 2)] = short_conv(c, 0)

    def gate(c):
        lanes = pl.ds(pl.multiple_of(c * width, width), width)
        for k in range(1, seqs):
            tap_arrival(c, k).wait_recv()
        f_high, f_low = forward_ref[0], forward_ref[1]
        i_high, i_low = inverse_ref[0], inverse_ref[1]
        h = taps[c]
        spectrum = dot(f_high[:, :half], h) + dot(f_low[:, :half], h)
        skip = skip_ref[pl.ds(0, 1), lanes]
        first = lax.broadcasted_iota(jnp.int32, (half, width), 0) == 0
        h_real = spectrum[:half] + skip
        h_imag = jnp.where(first, 0.0, spectrum[half:])
        h_last = jnp.where(first, spectrum[half:] + skip, h_real)

        def block(before, now):
            window = jnp.concatenate([before, now], 0)
            x = dot(f_high, window) + dot(f_low, window)
            a, b = x[:half], x[half:]
            y = jnp.concatenate([a * h_real - b * h_imag, a * h_imag + b * h_last], 0)
            y_high = y.astype(BF16)
            y_low = (y - y_high.astype(F32)).astype(BF16)
            return dot(i_high, y_high) + dot(i_low, y_high) + dot(i_high, y_low)

        slot = lax.rem(c, 2)
        upper = block(prod[c, 0:half, :], prod[c, half:, :])
        gath[p, c, pl.ds(half, half), :] = (query[slot, pl.ds(half, half), :] * upper).astype(BF16)

        @pl.when(s > 0)
        def _():
            ph_copy(c).wait_recv()

        lower = block(phalo[c], prod[c, 0:half, :])
        gath[p, c, pl.ds(0, half), :] = (query[slot, pl.ds(0, half), :] * lower).astype(BF16)
        for way in range(2):
            g_copy(p, c, way).start()

    def pass_on(c):
        for way in range(2):
            g_copy(beside[way], c, way).wait_recv()
            d_copy(beside[way], c, way).start()

    tile = 512

    def project(c, owners):
        for q in owners:
            w_copy(q, c).wait()

        @pl.loop(0, channels // tile)
        def _(n):
            lanes = pl.ds(pl.multiple_of(n * tile, tile), tile)
            total = acc[:, lanes]
            for q in owners:
                total = total + dot(gath[q, c], wbuf[q, c, :, lanes])
            acc[:, lanes] = total

    @pl.loop(0, chunks + 4)
    def _(i):
        @pl.when(i + ahead < chunks)
        def _():
            share(i + ahead)

        @pl.when(i < chunks)
        def _():
            products(i)

        @pl.when((i >= 1) & (i < chunks + 1))
        def _():
            gate(i - 1)

        @pl.when((i >= 3) & (i < chunks + 3))
        def _():
            pass_on(i - 3)
            project(i - 3, (p,) + beside)

        @pl.when(i >= 4)
        def _():
            for way in range(2):
                d_copy(across, i - 4, way).wait_recv()
            project(i - 4, (across,))

    out_ref[...] = acc[...].astype(BF16)

    @pl.loop(0, chunks)
    def _(c):
        @pl.when(s < seqs - 1)
        def _():
            fh_copy(c).wait_send()
            ph_copy(c).wait_send()

        for k in range(1, seqs):
            tap_copy(c, k).wait_send()
        for way in range(2):
            g_copy(p, c, way).wait_send()
            d_copy(beside[way], c, way).wait_send()


def fused(seqs, tps, features, short_filter, medium_filter, skip_gain, out_weight):
    _, rows, channels = features.shape
    own_taps = medium_filter.shape[0]
    short = short_filter.shape[0]
    width = 256
    chunks = channels // width
    edge = 16
    forward, inverse = transforms(rows)
    sizes = (seqs, tps, chunks, width, rows, channels, own_taps, short)
    vmem = pl.BlockSpec(memory_space=pltpu.VMEM)
    anywhere = pl.BlockSpec(memory_space=pl.ANY)
    dma = pltpu.SemaphoreType.DMA
    columns = out_weight.shape[1]
    return pl.pallas_call(
        functools.partial(kernel, sizes),
        out_shape=jax.ShapeDtypeStruct((rows, columns), BF16),
        in_specs=[anywhere, vmem, vmem, vmem, vmem, vmem, anywhere],
        out_specs=vmem,
        scratch_shapes=[
            pltpu.VMEM((chunks, 3, rows, width), BF16),
            pltpu.VMEM((chunks, 3, edge, width), BF16),
            pltpu.VMEM((3, rows + 8, width), F32),
            pltpu.VMEM((2, rows, width), F32),
            pltpu.VMEM((chunks, rows, width), BF16),
            pltpu.VMEM((chunks, rows // 2, width), BF16),
            pltpu.VMEM((chunks, seqs * own_taps, width), BF16),
            pltpu.VMEM((tps, chunks, rows, width), BF16),
            pltpu.VMEM((tps, chunks, width, columns), BF16),
            pltpu.VMEM((rows, columns), F32),
            dma((chunks,)),
            dma((tps, chunks)),
            dma((chunks,)),
            dma((chunks,)),
            dma((chunks,)),
            dma((chunks,)),
            dma((chunks, seqs - 1)),
            dma((chunks, seqs - 1)),
            dma((chunks, 2)),
            dma((chunks, 2)),
            dma((chunks, 2)),
            dma((chunks, 2)),
        ],
        compiler_params=pltpu.CompilerParams(
            collective_id=0, has_side_effects=True, vmem_limit_bytes=56 * 1024 * 1024
        ),
    )(
        features,
        short_filter.transpose(1, 0, 2),
        medium_filter,
        skip_gain.reshape(1, channels),
        jnp.asarray(forward),
        jnp.asarray(inverse),
        out_weight,
    )


def solution(mesh):
    in_specs = (P(None, "seq", "tp"), P(None, None, "tp"), P("seq", "tp"), P("tp"), P(None, "tp"))
    out_specs = P("seq", "tp")
    seqs, tps = mesh.shape["seq"], mesh.shape["tp"]

    def body(features, short_filter, medium_filter, skip_gain, out_weight):
        taps_all = seqs * medium_filter.shape[0]
        fits = (
            tps == 4
            and seqs > 1
            and medium_filter.shape[0] % 16 == 0
            and features.shape[1] == 2 * taps_all
            and features.shape[2] % 512 == 0
            and short_filter.shape[0] <= 9
        )
        if fits:
            return fused(
                seqs, tps, features, short_filter, medium_filter, skip_gain, out_weight
            )
        return on_device(features, short_filter, medium_filter, skip_gain, out_weight)

    return jax.shard_map(body, mesh=mesh, in_specs=in_specs, out_specs=out_specs, check_vma=False)
```

```python
import functools

import jax
import jax.numpy as jnp
import ml_dtypes
import numpy as np
from jax import lax
from jax.experimental import pallas as pl
from jax.experimental.pallas import tpu as pltpu
from jax.sharding import PartitionSpec as P

MESH = pl.DeviceIdType.MESH
F32 = jnp.float32
BF16 = jnp.bfloat16


def passed_along(value, axis, steps):
    count = lax.axis_size(axis)
    leading, last = (max(0, -steps), min(count, count - steps))
    return lax.ppermute(value, axis, [(source, source + steps) for source in range(leading, last)])


def depthwise(extended, kernel):
    channels = extended.shape[1]
    return lax.conv_general_dilated(
        extended[None],
        kernel[::-1][:, None, :],
        (1,),
        "VALID",
        dimension_numbers=("NWC", "WIO", "NWC"),
        feature_group_count=channels,
        precision=lax.Precision.HIGHEST,
    )[0]


def on_device(features, short_filter, medium_filter, skip_gain, out_weight):
    taps_full = lax.all_gather(medium_filter, "seq", axis=0, tiled=True)
    long_reach = taps_full.shape[0]
    short_reach = short_filter.shape[0]
    tok_rows = features.shape[1]
    lead_rows = passed_along(features[:, tok_rows - (short_reach - 1) :, :], "seq", 1)
    extended = jnp.concatenate([lead_rows, features], 1).astype(F32)
    query_conv = depthwise(extended[0], short_filter[:, 0, :])
    key_conv = depthwise(extended[1], short_filter[:, 1, :])
    value_conv = depthwise(extended[2], short_filter[:, 2, :])
    product = (key_conv * value_conv).astype(BF16)
    lead_product = passed_along(product[tok_rows - (long_reach - 1) :], "seq", 1)
    product_ext = jnp.concatenate([lead_product, product], 0)
    longer = depthwise(product_ext.astype(F32), taps_full)
    gated_rows = (query_conv * (longer + skip_gain * product.astype(F32))).astype(BF16)
    gathered = lax.all_gather(gated_rows, "tp", axis=1, tiled=True)
    result = jnp.dot(gathered, out_weight, preferred_element_type=F32)
    return result.astype(BF16)


def split(matrix):
    high = matrix.astype(ml_dtypes.bfloat16)
    low = (matrix - high.astype(np.float64)).astype(ml_dtypes.bfloat16)
    return np.stack([high, low])


def transforms(points):
    half = points // 2
    at = np.arange(points)
    angle = 2 * np.pi * ((np.arange(half)[:, None] * at[None, :]) % points) / points
    real, imag = np.cos(angle), -np.sin(angle)
    imag[0] = np.where(at % 2 == 0, 1.0, -1.0)
    forward = np.concatenate([real, imag], 0)
    weight = np.full((points, 1), 2.0 / points)
    weight[0] = weight[half] = 1.0 / points
    inverse = (forward * weight).T[half:]
    return split(forward), split(inverse)


def dot(a, b):
    return jnp.dot(a, b, preferred_element_type=F32)


def kernel(
    sizes,
    features,
    short_ref,
    medium_ref,
    skip_ref,
    forward_ref,
    inverse_ref,
    weight,
    out_ref,
    feat,
    fhalo,
    ext,
    query,
    prod,
    phalo,
    taps,
    gath,
    wbuf,
    acc,
    feat_sem,
    w_sem,
    fh_send,
    fh_recv,
    ph_send,
    ph_recv,
    tap_send,
    tap_recv,
    g_send,
    g_recv,
    d_send,
    d_recv,
):
    seqs, tps, chunks, width, rows, channels, own_taps, short = sizes
    half = rows // 2
    edge = 16
    s = lax.axis_index("seq")
    p = lax.axis_index("tp")
    beside = (p + 1 - 2 * lax.rem(p, 2), lax.rem(p + 2, 4))
    across = 3 - p

    def feat_copy(c):
        return pltpu.make_async_copy(
            features.at[:, :, pl.ds(pl.multiple_of(c * width, width), width)],
            feat.at[c],
            feat_sem.at[c],
        )

    def w_copy(q, c):
        first = pl.multiple_of(q * channels + c * width, width)
        return pltpu.make_async_copy(
            weight.at[pl.ds(first, width), :], wbuf.at[q, c], w_sem.at[q, c]
        )

    def fh_copy(c):
        return pltpu.make_async_remote_copy(
            src_ref=feat.at[c, :, pl.ds(rows - edge, edge), :],
            dst_ref=fhalo.at[c],
            send_sem=fh_send.at[c],
            recv_sem=fh_recv.at[c],
            device_id=(s + 1, p),
            device_id_type=MESH,
        )

    def ph_copy(c):
        return pltpu.make_async_remote_copy(
            src_ref=prod.at[c, pl.ds(half, half), :],
            dst_ref=phalo.at[c],
            send_sem=ph_send.at[c],
            recv_sem=ph_recv.at[c],
            device_id=(s + 1, p),
            device_id_type=MESH,
        )

    def tap_copy(c, k):
        mine = pl.ds(pl.multiple_of(s * own_taps, own_taps), own_taps)
        return pltpu.make_async_remote_copy(
            src_ref=taps.at[c, mine, :],
            dst_ref=taps.at[c, mine, :],
            send_sem=tap_send.at[c, k - 1],
            recv_sem=tap_recv.at[c, k - 1],
            device_id=(lax.rem(s + k, seqs), p),
            device_id_type=MESH,
        )

    def tap_arrival(c, k):
        other = lax.rem(s + seqs - k, seqs)
        theirs = pl.ds(pl.multiple_of(other * own_taps, own_taps), own_taps)
        return pltpu.make_async_remote_copy(
            src_ref=taps.at[c, theirs, :],
            dst_ref=taps.at[c, theirs, :],
            send_sem=tap_send.at[c, k - 1],
            recv_sem=tap_recv.at[c, k - 1],
            device_id=(other, p),
            device_id_type=MESH,
        )

    def g_copy(owner, c, way):
        return pltpu.make_async_remote_copy(
            src_ref=gath.at[owner, c],
            dst_ref=gath.at[owner, c],
            send_sem=g_send.at[c, way],
            recv_sem=g_recv.at[c, way],
            device_id=(s, beside[way]),
            device_id_type=MESH,
        )

    def d_copy(owner, c, way):
        piece = pl.ds(way * half, half)
        return pltpu.make_async_remote_copy(
            src_ref=gath.at[owner, c, piece, :],
            dst_ref=gath.at[owner, c, piece, :],
            send_sem=d_send.at[c, way],
            recv_sem=d_recv.at[c, way],
            device_id=(s, beside[1 - way]),
            device_id_type=MESH,
        )

    for c in range(chunks):
        feat_copy(c).start()
    barrier = pltpu.get_barrier_semaphore()
    for k in range(1, seqs):
        pl.semaphore_signal(
            barrier, inc=1, device_id=(lax.rem(s + k, seqs), p), device_id_type=MESH
        )
    for way in range(2):
        pl.semaphore_signal(barrier, inc=1, device_id=(s, beside[way]), device_id_type=MESH)

    own = pl.ds(pl.multiple_of(s * own_taps, own_taps), own_taps)
    for c in range(chunks):
        taps[c, own, :] = medium_ref[:, c * width : (c + 1) * width].astype(BF16)

    @pl.when(s == 0)
    def _():
        fhalo[...] = jnp.zeros_like(fhalo)
        phalo[...] = jnp.zeros_like(phalo)

    def short_conv(c, stream, start):
        lanes = pl.ds(pl.multiple_of(c * width, width), width)
        total = None
        for j in range(short):
            piece = ext[stream, pl.ds(start + 8 - j, half), :]
            term = short_ref[stream, pl.ds(j, 1), lanes] * piece
            total = term if total is None else total + term
        return total

    def convolve(c, start):
        here = pl.ds(start, half)
        product = short_conv(c, 1, start) * short_conv(c, 2, start)
        prod[c, here, :] = product.astype(BF16)
        query[lax.rem(c, 2), here, :] = short_conv(c, 0, start)

    def later(c):
        for stream in range(3):
            ext[stream, 8:, :] = feat[c, stream, :, :].astype(F32)
        convolve(c, half)

    def earlier(c):
        @pl.when(s > 0)
        def _():
            fh_copy(c).wait_recv()

        for stream in range(3):
            ext[stream, 0:8, :] = fhalo[c, stream, :, :].astype(F32)[edge - 8 :]
        convolve(c, 0)

    def share(c):
        @pl.when(s < seqs - 1)
        def _():
            fh_copy(c).start()

        for k in range(1, seqs):
            tap_copy(c, k).start()

    def hand_on(c):
        @pl.when(s < seqs - 1)
        def _():
            ph_copy(c).start()

    feat_copy(0).wait()
    later(0)
    pl.semaphore_wait(barrier, seqs + 1)
    share(0)
    hand_on(0)

    @pl.loop(0, chunks)
    def _(c):
        for q in range(tps):
            w_copy(q, c).start()

    acc[...] = jnp.zeros_like(acc)

    def gate(c):
        lanes = pl.ds(pl.multiple_of(c * width, width), width)
        for k in range(1, seqs):
            tap_arrival(c, k).wait_recv()
        f_high, f_low = forward_ref[0], forward_ref[1]
        i_high, i_low = inverse_ref[0], inverse_ref[1]
        h = taps[c]
        spectrum = dot(f_high[:, :half], h) + dot(f_low[:, :half], h)
        skip = skip_ref[pl.ds(0, 1), lanes]
        first = lax.broadcasted_iota(jnp.int32, (half, width), 0) == 0
        h_real = spectrum[:half] + skip
        h_imag = jnp.where(first, 0.0, spectrum[half:])
        h_last = jnp.where(first, spectrum[half:] + skip, h_real)

        def block(before, now):
            window = jnp.concatenate([before, now], 0)
            x = dot(f_high, window) + dot(f_low, window)
            a, b = x[:half], x[half:]
            y = jnp.concatenate([a * h_real - b * h_imag, a * h_imag + b * h_last], 0)
            y_high = y.astype(BF16)
            y_low = (y - y_high.astype(F32)).astype(BF16)
            return dot(i_high, y_high) + dot(i_low, y_high) + dot(i_high, y_low)

        slot = lax.rem(c, 2)
        upper = block(prod[c, 0:half, :], prod[c, half:, :])
        gath[p, c, pl.ds(half, half), :] = (query[slot, pl.ds(half, half), :] * upper).astype(BF16)

        @pl.when(s > 0)
        def _():
            ph_copy(c).wait_recv()

        lower = block(phalo[c], prod[c, 0:half, :])
        gath[p, c, pl.ds(0, half), :] = (query[slot, pl.ds(0, half), :] * lower).astype(BF16)
        for way in range(2):
            g_copy(p, c, way).start()

    def pass_on(c):
        for way in range(2):
            g_copy(beside[way], c, way).wait_recv()
            d_copy(beside[way], c, way).start()

    tile = 512

    def project(c, owners):
        for q in owners:
            w_copy(q, c).wait()

        @pl.loop(0, channels // tile)
        def _(n):
            lanes = pl.ds(pl.multiple_of(n * tile, tile), tile)
            total = acc[:, lanes]
            for q in owners:
                total = total + dot(gath[q, c], wbuf[q, c, :, lanes])
            acc[:, lanes] = total

    @pl.loop(0, chunks + 3)
    def _(i):
        @pl.when(i + 1 < chunks)
        def _():
            feat_copy(i + 1).wait()
            share(i + 1)

        @pl.when(i < chunks)
        def _():
            earlier(i)

        @pl.when(i + 1 < chunks)
        def _():
            later(i + 1)
            hand_on(i + 1)

        @pl.when(i < chunks)
        def _():
            gate(i)

        @pl.when((i >= 2) & (i < chunks + 2))
        def _():
            pass_on(i - 2)
            project(i - 2, (p,) + beside)

        @pl.when(i >= 3)
        def _():
            for way in range(2):
                d_copy(across, i - 3, way).wait_recv()
            project(i - 3, (across,))

    out_ref[...] = acc[...].astype(BF16)

    @pl.loop(0, chunks)
    def _(c):
        @pl.when(s < seqs - 1)
        def _():
            fh_copy(c).wait_send()
            ph_copy(c).wait_send()

        for k in range(1, seqs):
            tap_copy(c, k).wait_send()
        for way in range(2):
            g_copy(p, c, way).wait_send()
            d_copy(beside[way], c, way).wait_send()


def fused(seqs, tps, features, short_filter, medium_filter, skip_gain, out_weight):
    _, rows, channels = features.shape
    own_taps = medium_filter.shape[0]
    short = short_filter.shape[0]
    width = 256
    chunks = channels // width
    edge = 16
    forward, inverse = transforms(rows)
    sizes = (seqs, tps, chunks, width, rows, channels, own_taps, short)
    vmem = pl.BlockSpec(memory_space=pltpu.VMEM)
    anywhere = pl.BlockSpec(memory_space=pl.ANY)
    dma = pltpu.SemaphoreType.DMA
    columns = out_weight.shape[1]
    return pl.pallas_call(
        functools.partial(kernel, sizes),
        out_shape=jax.ShapeDtypeStruct((rows, columns), BF16),
        in_specs=[anywhere, vmem, vmem, vmem, vmem, vmem, anywhere],
        out_specs=vmem,
        scratch_shapes=[
            pltpu.VMEM((chunks, 3, rows, width), BF16),
            pltpu.VMEM((chunks, 3, edge, width), BF16),
            pltpu.VMEM((3, rows + 8, width), F32),
            pltpu.VMEM((2, rows, width), F32),
            pltpu.VMEM((chunks, rows, width), BF16),
            pltpu.VMEM((chunks, rows // 2, width), BF16),
            pltpu.VMEM((chunks, seqs * own_taps, width), BF16),
            pltpu.VMEM((tps, chunks, rows, width), BF16),
            pltpu.VMEM((tps, chunks, width, columns), BF16),
            pltpu.VMEM((rows, columns), F32),
            dma((chunks,)),
            dma((tps, chunks)),
            dma((chunks,)),
            dma((chunks,)),
            dma((chunks,)),
            dma((chunks,)),
            dma((chunks, seqs - 1)),
            dma((chunks, seqs - 1)),
            dma((chunks, 2)),
            dma((chunks, 2)),
            dma((chunks, 2)),
            dma((chunks, 2)),
        ],
        compiler_params=pltpu.CompilerParams(
            collective_id=0, has_side_effects=True, vmem_limit_bytes=56 * 1024 * 1024
        ),
    )(
        features,
        short_filter.transpose(1, 0, 2),
        medium_filter,
        skip_gain.reshape(1, channels),
        jnp.asarray(forward),
        jnp.asarray(inverse),
        out_weight,
    )


def solution(mesh):
    in_specs = (P(None, "seq", "tp"), P(None, None, "tp"), P("seq", "tp"), P("tp"), P(None, "tp"))
    out_specs = P("seq", "tp")
    seqs, tps = mesh.shape["seq"], mesh.shape["tp"]

    def body(features, short_filter, medium_filter, skip_gain, out_weight):
        taps_all = seqs * medium_filter.shape[0]
        fits = (
            tps == 4
            and seqs > 1
            and medium_filter.shape[0] % 16 == 0
            and features.shape[1] == 2 * taps_all
            and features.shape[2] % 512 == 0
            and short_filter.shape[0] <= 9
        )
        if fits:
            return fused(
                seqs, tps, features, short_filter, medium_filter, skip_gain, out_weight
            )
        return on_device(features, short_filter, medium_filter, skip_gain, out_weight)

    return jax.shard_map(body, mesh=mesh, in_specs=in_specs, out_specs=out_specs, check_vma=False)
```

```python
import functools

import jax
import jax.numpy as jnp
import ml_dtypes
import numpy as np
from jax import lax
from jax.experimental import pallas as pl
from jax.experimental.pallas import tpu as pltpu
from jax.sharding import PartitionSpec as P

MESH = pl.DeviceIdType.MESH
F32 = jnp.float32
BF16 = jnp.bfloat16


def passed_along(value, axis, steps):
    count = lax.axis_size(axis)
    leading, last = (max(0, -steps), min(count, count - steps))
    return lax.ppermute(value, axis, [(source, source + steps) for source in range(leading, last)])


def depthwise(extended, kernel):
    channels = extended.shape[1]
    return lax.conv_general_dilated(
        extended[None],
        kernel[::-1][:, None, :],
        (1,),
        "VALID",
        dimension_numbers=("NWC", "WIO", "NWC"),
        feature_group_count=channels,
        precision=lax.Precision.HIGHEST,
    )[0]


def on_device(features, short_filter, medium_filter, skip_gain, out_weight):
    taps_full = lax.all_gather(medium_filter, "seq", axis=0, tiled=True)
    long_reach = taps_full.shape[0]
    short_reach = short_filter.shape[0]
    tok_rows = features.shape[1]
    lead_rows = passed_along(features[:, tok_rows - (short_reach - 1) :, :], "seq", 1)
    extended = jnp.concatenate([lead_rows, features], 1).astype(F32)
    query_conv = depthwise(extended[0], short_filter[:, 0, :])
    key_conv = depthwise(extended[1], short_filter[:, 1, :])
    value_conv = depthwise(extended[2], short_filter[:, 2, :])
    product = (key_conv * value_conv).astype(BF16)
    lead_product = passed_along(product[tok_rows - (long_reach - 1) :], "seq", 1)
    product_ext = jnp.concatenate([lead_product, product], 0)
    longer = depthwise(product_ext.astype(F32), taps_full)
    gated_rows = (query_conv * (longer + skip_gain * product.astype(F32))).astype(BF16)
    gathered = lax.all_gather(gated_rows, "tp", axis=1, tiled=True)
    result = jnp.dot(gathered, out_weight, preferred_element_type=F32)
    return result.astype(BF16)


def split(matrix):
    high = matrix.astype(ml_dtypes.bfloat16)
    low = (matrix - high.astype(np.float64)).astype(ml_dtypes.bfloat16)
    return np.stack([high, low])


def transforms(points):
    half = points // 2
    at = np.arange(points)
    angle = 2 * np.pi * ((np.arange(half)[:, None] * at[None, :]) % points) / points
    real, imag = np.cos(angle), -np.sin(angle)
    imag[0] = np.where(at % 2 == 0, 1.0, -1.0)
    forward = np.concatenate([real, imag], 0)
    weight = np.full((points, 1), 2.0 / points)
    weight[0] = weight[half] = 1.0 / points
    inverse = (forward * weight).T[half:]
    return split(forward), split(inverse)


def dot(a, b):
    return jnp.dot(a, b, preferred_element_type=F32)


def kernel(
    sizes,
    features,
    short_ref,
    medium_ref,
    skip_ref,
    forward_ref,
    inverse_ref,
    weight,
    out_ref,
    feat,
    fhalo,
    ext,
    query,
    prod,
    phalo,
    taps,
    gath,
    wbuf,
    acc,
    feat_sem,
    w_sem,
    fh_send,
    fh_recv,
    ph_send,
    ph_recv,
    tap_send,
    tap_recv,
    g_send,
    g_recv,
    d_send,
    d_recv,
):
    seqs, tps, chunks, width, rows, channels, own_taps, short = sizes
    half = rows // 2
    edge = 16
    s = lax.axis_index("seq")
    p = lax.axis_index("tp")
    beside = (p + 1 - 2 * lax.rem(p, 2), lax.rem(p + 2, 4))
    across = 3 - p

    def feat_copy(c):
        return pltpu.make_async_copy(
            features.at[:, :, pl.ds(pl.multiple_of(c * width, width), width)],
            feat.at[c],
            feat_sem.at[c],
        )

    def w_copy(q, c):
        first = pl.multiple_of(q * channels + c * width, width)
        return pltpu.make_async_copy(
            weight.at[pl.ds(first, width), :], wbuf.at[q, c], w_sem.at[q, c]
        )

    def fh_copy(c):
        return pltpu.make_async_remote_copy(
            src_ref=feat.at[c, :, pl.ds(rows - edge, edge), :],
            dst_ref=fhalo.at[c],
            send_sem=fh_send.at[c],
            recv_sem=fh_recv.at[c],
            device_id=(s + 1, p),
            device_id_type=MESH,
        )

    def ph_copy(c):
        return pltpu.make_async_remote_copy(
            src_ref=prod.at[c, pl.ds(half, half), :],
            dst_ref=phalo.at[c],
            send_sem=ph_send.at[c],
            recv_sem=ph_recv.at[c],
            device_id=(s + 1, p),
            device_id_type=MESH,
        )

    def tap_copy(c, k):
        mine = pl.ds(pl.multiple_of(s * own_taps, own_taps), own_taps)
        return pltpu.make_async_remote_copy(
            src_ref=taps.at[c, mine, :],
            dst_ref=taps.at[c, mine, :],
            send_sem=tap_send.at[c, k - 1],
            recv_sem=tap_recv.at[c, k - 1],
            device_id=(lax.rem(s + k, seqs), p),
            device_id_type=MESH,
        )

    def tap_arrival(c, k):
        other = lax.rem(s + seqs - k, seqs)
        theirs = pl.ds(pl.multiple_of(other * own_taps, own_taps), own_taps)
        return pltpu.make_async_remote_copy(
            src_ref=taps.at[c, theirs, :],
            dst_ref=taps.at[c, theirs, :],
            send_sem=tap_send.at[c, k - 1],
            recv_sem=tap_recv.at[c, k - 1],
            device_id=(other, p),
            device_id_type=MESH,
        )

    def g_copy(owner, c, way, part):
        piece = pl.ds(part * half, half)
        return pltpu.make_async_remote_copy(
            src_ref=gath.at[owner, c, piece, :],
            dst_ref=gath.at[owner, c, piece, :],
            send_sem=g_send.at[c, 2 * way + part],
            recv_sem=g_recv.at[c, 2 * way + part],
            device_id=(s, beside[way]),
            device_id_type=MESH,
        )

    def d_copy(owner, c, way):
        piece = pl.ds(way * half, half)
        return pltpu.make_async_remote_copy(
            src_ref=gath.at[owner, c, piece, :],
            dst_ref=gath.at[owner, c, piece, :],
            send_sem=d_send.at[c, way],
            recv_sem=d_recv.at[c, way],
            device_id=(s, beside[1 - way]),
            device_id_type=MESH,
        )

    for c in range(chunks):
        feat_copy(c).start()
    barrier = pltpu.get_barrier_semaphore()
    for k in range(1, seqs):
        pl.semaphore_signal(
            barrier, inc=1, device_id=(lax.rem(s + k, seqs), p), device_id_type=MESH
        )
    for way in range(2):
        pl.semaphore_signal(barrier, inc=1, device_id=(s, beside[way]), device_id_type=MESH)

    own = pl.ds(pl.multiple_of(s * own_taps, own_taps), own_taps)
    for c in range(chunks):
        taps[c, own, :] = medium_ref[:, c * width : (c + 1) * width].astype(BF16)

    @pl.when(s == 0)
    def _():
        fhalo[...] = jnp.zeros_like(fhalo)
        phalo[...] = jnp.zeros_like(phalo)

    def short_conv(c, stream, start):
        lanes = pl.ds(pl.multiple_of(c * width, width), width)
        total = None
        for j in range(short):
            piece = ext[stream, pl.ds(start + 8 - j, half), :]
            term = short_ref[stream, pl.ds(j, 1), lanes] * piece
            total = term if total is None else total + term
        return total

    def convolve(c, start):
        here = pl.ds(start, half)
        product = short_conv(c, 1, start) * short_conv(c, 2, start)
        prod[c, here, :] = product.astype(BF16)
        query[lax.rem(c, 2), here, :] = short_conv(c, 0, start)

    def later(c):
        for stream in range(3):
            ext[stream, 8:, :] = feat[c, stream, :, :].astype(F32)
        convolve(c, half)

    def earlier(c):
        @pl.when(s > 0)
        def _():
            fh_copy(c).wait_recv()

        for stream in range(3):
            ext[stream, 0:8, :] = fhalo[c, stream, :, :].astype(F32)[edge - 8 :]
        convolve(c, 0)

    def share(c):
        @pl.when(s < seqs - 1)
        def _():
            fh_copy(c).start()

        for k in range(1, seqs):
            tap_copy(c, k).start()

    def hand_on(c):
        @pl.when(s < seqs - 1)
        def _():
            ph_copy(c).start()

    feat_copy(0).wait()
    later(0)
    pl.semaphore_wait(barrier, seqs + 1)
    share(0)
    hand_on(0)

    @pl.loop(0, chunks)
    def _(c):
        for q in range(tps):
            w_copy(q, c).start()

    acc[...] = jnp.zeros_like(acc)

    def gate(c):
        lanes = pl.ds(pl.multiple_of(c * width, width), width)
        for k in range(1, seqs):
            tap_arrival(c, k).wait_recv()
        f_high, f_low = forward_ref[0], forward_ref[1]
        i_high, i_low = inverse_ref[0], inverse_ref[1]
        h = taps[c]
        spectrum = dot(f_high[:, :half], h) + dot(f_low[:, :half], h)
        skip = skip_ref[pl.ds(0, 1), lanes]
        first = lax.broadcasted_iota(jnp.int32, (half, width), 0) == 0
        h_real = spectrum[:half] + skip
        h_imag = jnp.where(first, 0.0, spectrum[half:])
        h_last = jnp.where(first, spectrum[half:] + skip, h_real)

        def block(before, now):
            window = jnp.concatenate([before, now], 0)
            x = dot(f_high, window) + dot(f_low, window)
            a, b = x[:half], x[half:]
            y = jnp.concatenate([a * h_real - b * h_imag, a * h_imag + b * h_last], 0)
            y_high = y.astype(BF16)
            y_low = (y - y_high.astype(F32)).astype(BF16)
            return dot(i_high, y_high) + dot(i_low, y_high) + dot(i_high, y_low)

        slot = lax.rem(c, 2)
        upper = block(prod[c, 0:half, :], prod[c, half:, :])
        gath[p, c, pl.ds(half, half), :] = (query[slot, pl.ds(half, half), :] * upper).astype(BF16)
        for way in range(2):
            g_copy(p, c, way, 1).start()

        @pl.when(s > 0)
        def _():
            ph_copy(c).wait_recv()

        lower = block(phalo[c], prod[c, 0:half, :])
        gath[p, c, pl.ds(0, half), :] = (query[slot, pl.ds(0, half), :] * lower).astype(BF16)
        for way in range(2):
            g_copy(p, c, way, 0).start()

    def pass_on(c):
        for way in (1, 0):
            g_copy(beside[way], c, way, way).wait_recv()
            d_copy(beside[way], c, way).start()
        for way in (0, 1):
            g_copy(beside[way], c, way, 1 - way).wait_recv()

    tile = 1024

    def project(c, owners):
        for q in owners:
            w_copy(q, c).wait()

        @pl.loop(0, channels // tile)
        def _(n):
            lanes = pl.ds(pl.multiple_of(n * tile, tile), tile)
            total = acc[:, lanes]
            for q in owners:
                total = total + dot(gath[q, c], wbuf[q, c, :, lanes])
            acc[:, lanes] = total

    @pl.loop(0, chunks + 3)
    def _(i):
        @pl.when(i + 1 < chunks)
        def _():
            feat_copy(i + 1).wait()
            share(i + 1)

        @pl.when(i < chunks)
        def _():
            earlier(i)

        @pl.when(i + 1 < chunks)
        def _():
            later(i + 1)
            hand_on(i + 1)

        @pl.when(i < chunks)
        def _():
            gate(i)

        @pl.when((i >= 2) & (i < chunks + 2))
        def _():
            pass_on(i - 2)
            project(i - 2, (p,) + beside)

        @pl.when(i >= 3)
        def _():
            for way in range(2):
                d_copy(across, i - 3, way).wait_recv()
            project(i - 3, (across,))

    out_ref[...] = acc[...].astype(BF16)

    @pl.loop(0, chunks)
    def _(c):
        @pl.when(s < seqs - 1)
        def _():
            fh_copy(c).wait_send()
            ph_copy(c).wait_send()

        for k in range(1, seqs):
            tap_copy(c, k).wait_send()
        for way in range(2):
            for part in range(2):
                g_copy(p, c, way, part).wait_send()
            d_copy(beside[way], c, way).wait_send()


def fused(seqs, tps, features, short_filter, medium_filter, skip_gain, out_weight):
    _, rows, channels = features.shape
    own_taps = medium_filter.shape[0]
    short = short_filter.shape[0]
    width = 256
    chunks = channels // width
    edge = 16
    forward, inverse = transforms(rows)
    sizes = (seqs, tps, chunks, width, rows, channels, own_taps, short)
    vmem = pl.BlockSpec(memory_space=pltpu.VMEM)
    anywhere = pl.BlockSpec(memory_space=pl.ANY)
    dma = pltpu.SemaphoreType.DMA
    columns = out_weight.shape[1]
    return pl.pallas_call(
        functools.partial(kernel, sizes),
        out_shape=jax.ShapeDtypeStruct((rows, columns), BF16),
        in_specs=[anywhere, vmem, vmem, vmem, vmem, vmem, anywhere],
        out_specs=vmem,
        scratch_shapes=[
            pltpu.VMEM((chunks, 3, rows, width), BF16),
            pltpu.VMEM((chunks, 3, edge, width), BF16),
            pltpu.VMEM((3, rows + 8, width), F32),
            pltpu.VMEM((2, rows, width), F32),
            pltpu.VMEM((chunks, rows, width), BF16),
            pltpu.VMEM((chunks, rows // 2, width), BF16),
            pltpu.VMEM((chunks, seqs * own_taps, width), BF16),
            pltpu.VMEM((tps, chunks, rows, width), BF16),
            pltpu.VMEM((tps, chunks, width, columns), BF16),
            pltpu.VMEM((rows, columns), F32),
            dma((chunks,)),
            dma((tps, chunks)),
            dma((chunks,)),
            dma((chunks,)),
            dma((chunks,)),
            dma((chunks,)),
            dma((chunks, seqs - 1)),
            dma((chunks, seqs - 1)),
            dma((chunks, 4)),
            dma((chunks, 4)),
            dma((chunks, 2)),
            dma((chunks, 2)),
        ],
        compiler_params=pltpu.CompilerParams(
            collective_id=0, has_side_effects=True, vmem_limit_bytes=56 * 1024 * 1024
        ),
    )(
        features,
        short_filter.transpose(1, 0, 2),
        medium_filter,
        skip_gain.reshape(1, channels),
        jnp.asarray(forward),
        jnp.asarray(inverse),
        out_weight,
    )


def solution(mesh):
    in_specs = (P(None, "seq", "tp"), P(None, None, "tp"), P("seq", "tp"), P("tp"), P(None, "tp"))
    out_specs = P("seq", "tp")
    seqs, tps = mesh.shape["seq"], mesh.shape["tp"]

    def body(features, short_filter, medium_filter, skip_gain, out_weight):
        taps_all = seqs * medium_filter.shape[0]
        fits = (
            tps == 4
            and seqs > 1
            and medium_filter.shape[0] % 16 == 0
            and features.shape[1] == 2 * taps_all
            and features.shape[2] % 1024 == 0
            and short_filter.shape[0] <= 9
        )
        if fits:
            return fused(
                seqs, tps, features, short_filter, medium_filter, skip_gain, out_weight
            )
        return on_device(features, short_filter, medium_filter, skip_gain, out_weight)

    return jax.shard_map(body, mesh=mesh, in_specs=in_specs, out_specs=out_specs, check_vma=False)
```

```python
import functools

import jax
import jax.numpy as jnp
import ml_dtypes
import numpy as np
from jax import lax
from jax.experimental import pallas as pl
from jax.experimental.pallas import tpu as pltpu
from jax.sharding import PartitionSpec as P

MESH = pl.DeviceIdType.MESH
F32 = jnp.float32
BF16 = jnp.bfloat16


def passed_along(value, axis, steps):
    count = lax.axis_size(axis)
    leading, last = (max(0, -steps), min(count, count - steps))
    return lax.ppermute(value, axis, [(source, source + steps) for source in range(leading, last)])


def depthwise(extended, kernel):
    channels = extended.shape[1]
    return lax.conv_general_dilated(
        extended[None],
        kernel[::-1][:, None, :],
        (1,),
        "VALID",
        dimension_numbers=("NWC", "WIO", "NWC"),
        feature_group_count=channels,
        precision=lax.Precision.HIGHEST,
    )[0]


def on_device(features, short_filter, medium_filter, skip_gain, out_weight):
    taps_full = lax.all_gather(medium_filter, "seq", axis=0, tiled=True)
    long_reach = taps_full.shape[0]
    short_reach = short_filter.shape[0]
    tok_rows = features.shape[1]
    lead_rows = passed_along(features[:, tok_rows - (short_reach - 1) :, :], "seq", 1)
    extended = jnp.concatenate([lead_rows, features], 1).astype(F32)
    query_conv = depthwise(extended[0], short_filter[:, 0, :])
    key_conv = depthwise(extended[1], short_filter[:, 1, :])
    value_conv = depthwise(extended[2], short_filter[:, 2, :])
    product = (key_conv * value_conv).astype(BF16)
    lead_product = passed_along(product[tok_rows - (long_reach - 1) :], "seq", 1)
    product_ext = jnp.concatenate([lead_product, product], 0)
    longer = depthwise(product_ext.astype(F32), taps_full)
    gated_rows = (query_conv * (longer + skip_gain * product.astype(F32))).astype(BF16)
    gathered = lax.all_gather(gated_rows, "tp", axis=1, tiled=True)
    result = jnp.dot(gathered, out_weight, preferred_element_type=F32)
    return result.astype(BF16)


def split(matrix):
    high = matrix.astype(ml_dtypes.bfloat16)
    low = (matrix - high.astype(np.float64)).astype(ml_dtypes.bfloat16)
    return np.stack([high, low])


def transforms(points):
    half = points // 2
    at = np.arange(points)
    angle = 2 * np.pi * ((np.arange(half)[:, None] * at[None, :]) % points) / points
    real, imag = np.cos(angle), -np.sin(angle)
    imag[0] = np.where(at % 2 == 0, 1.0, -1.0)
    forward = np.concatenate([real, imag], 0)
    weight = np.full((points, 1), 2.0 / points)
    weight[0] = weight[half] = 1.0 / points
    inverse = (forward * weight).T[half:]
    return split(forward), split(inverse)


def dot(a, b):
    return jnp.dot(a, b, preferred_element_type=F32)


def kernel(
    sizes,
    features,
    short_ref,
    medium_ref,
    skip_ref,
    forward_ref,
    inverse_ref,
    weight,
    out_ref,
    feat,
    fhalo,
    ext,
    query,
    prod,
    phalo,
    taps,
    gath,
    wbuf,
    acc,
    feat_sem,
    w_sem,
    fh_send,
    fh_recv,
    ph_send,
    ph_recv,
    tap_send,
    tap_recv,
    g_send,
    g_recv,
    d_send,
    d_recv,
):
    seqs, tps, chunks, width, rows, channels, own_taps, short = sizes
    half = rows // 2
    edge = 16
    s = lax.axis_index("seq")
    p = lax.axis_index("tp")
    beside = (p + 1 - 2 * lax.rem(p, 2), lax.rem(p + 2, 4))
    across = 3 - p

    def feat_copy(c):
        return pltpu.make_async_copy(
            features.at[:, :, pl.ds(pl.multiple_of(c * width, width), width)],
            feat.at[c],
            feat_sem.at[c],
        )

    def w_copy(q, c):
        first = pl.multiple_of(q * channels + c * width, width)
        return pltpu.make_async_copy(
            weight.at[pl.ds(first, width), :], wbuf.at[q, c], w_sem.at[q, c]
        )

    def fh_copy(c):
        return pltpu.make_async_remote_copy(
            src_ref=feat.at[c, :, pl.ds(rows - edge, edge), :],
            dst_ref=fhalo.at[c],
            send_sem=fh_send.at[c],
            recv_sem=fh_recv.at[c],
            device_id=(s + 1, p),
            device_id_type=MESH,
        )

    def ph_copy(c):
        return pltpu.make_async_remote_copy(
            src_ref=prod.at[c, pl.ds(half, half), :],
            dst_ref=phalo.at[c],
            send_sem=ph_send.at[c],
            recv_sem=ph_recv.at[c],
            device_id=(s + 1, p),
            device_id_type=MESH,
        )

    def tap_copy(c, k):
        mine = pl.ds(pl.multiple_of(s * own_taps, own_taps), own_taps)
        return pltpu.make_async_remote_copy(
            src_ref=taps.at[c, mine, :],
            dst_ref=taps.at[c, mine, :],
            send_sem=tap_send.at[c, k - 1],
            recv_sem=tap_recv.at[c, k - 1],
            device_id=(lax.rem(s + k, seqs), p),
            device_id_type=MESH,
        )

    def tap_arrival(c, k):
        other = lax.rem(s + seqs - k, seqs)
        theirs = pl.ds(pl.multiple_of(other * own_taps, own_taps), own_taps)
        return pltpu.make_async_remote_copy(
            src_ref=taps.at[c, theirs, :],
            dst_ref=taps.at[c, theirs, :],
            send_sem=tap_send.at[c, k - 1],
            recv_sem=tap_recv.at[c, k - 1],
            device_id=(other, p),
            device_id_type=MESH,
        )

    def g_copy(owner, c, way, part):
        piece = pl.ds(part * half, half)
        return pltpu.make_async_remote_copy(
            src_ref=gath.at[owner, c, piece, :],
            dst_ref=gath.at[owner, c, piece, :],
            send_sem=g_send.at[c, 2 * way + part],
            recv_sem=g_recv.at[c, 2 * way + part],
            device_id=(s, beside[way]),
            device_id_type=MESH,
        )

    def d_copy(owner, c, way):
        piece = pl.ds(way * half, half)
        return pltpu.make_async_remote_copy(
            src_ref=gath.at[owner, c, piece, :],
            dst_ref=gath.at[owner, c, piece, :],
            send_sem=d_send.at[c, way],
            recv_sem=d_recv.at[c, way],
            device_id=(s, beside[1 - way]),
            device_id_type=MESH,
        )

    for c in range(chunks):
        feat_copy(c).start()
    barrier = pltpu.get_barrier_semaphore()
    for k in range(1, seqs):
        pl.semaphore_signal(
            barrier, inc=1, device_id=(lax.rem(s + k, seqs), p), device_id_type=MESH
        )
    for way in range(2):
        pl.semaphore_signal(barrier, inc=1, device_id=(s, beside[way]), device_id_type=MESH)

    own = pl.ds(pl.multiple_of(s * own_taps, own_taps), own_taps)
    for c in range(chunks):
        taps[c, own, :] = medium_ref[:, c * width : (c + 1) * width].astype(BF16)

    @pl.when(s == 0)
    def _():
        fhalo[...] = jnp.zeros_like(fhalo)
        phalo[...] = jnp.zeros_like(phalo)

    def short_conv(c, stream, start):
        lanes = pl.ds(pl.multiple_of(c * width, width), width)
        total = None
        for j in range(short):
            piece = ext[stream, pl.ds(start + 8 - j, half), :]
            term = short_ref[stream, pl.ds(j, 1), lanes] * piece
            total = term if total is None else total + term
        return total

    def convolve(c, start):
        here = pl.ds(start, half)
        product = short_conv(c, 1, start) * short_conv(c, 2, start)
        prod[c, here, :] = product.astype(BF16)
        query[lax.rem(c, 2), here, :] = short_conv(c, 0, start)

    def later(c):
        for stream in range(3):
            ext[stream, 8:, :] = feat[c, stream, :, :].astype(F32)
        convolve(c, half)

    def earlier(c):
        @pl.when(s > 0)
        def _():
            fh_copy(c).wait_recv()

        for stream in range(3):
            ext[stream, 0:8, :] = fhalo[c, stream, :, :].astype(F32)[edge - 8 :]
        convolve(c, 0)

    def share(c):
        @pl.when(s < seqs - 1)
        def _():
            fh_copy(c).start()

        for k in range(1, seqs):
            tap_copy(c, k).start()

    def hand_on(c):
        @pl.when(s < seqs - 1)
        def _():
            ph_copy(c).start()

    feat_copy(0).wait()
    later(0)
    pl.semaphore_wait(barrier, seqs + 1)
    share(0)
    hand_on(0)

    @pl.loop(0, chunks)
    def _(c):
        for q in range(tps):
            w_copy(q, c).start()

    acc[...] = jnp.zeros_like(acc)

    def gate(c):
        lanes = pl.ds(pl.multiple_of(c * width, width), width)
        for k in range(1, seqs):
            tap_arrival(c, k).wait_recv()
        f_high, f_low = forward_ref[0], forward_ref[1]
        i_high, i_low = inverse_ref[0], inverse_ref[1]
        h = taps[c]
        spectrum = dot(f_high[:, :half], h) + dot(f_low[:, :half], h)
        skip = skip_ref[pl.ds(0, 1), lanes]
        first = lax.broadcasted_iota(jnp.int32, (half, width), 0) == 0
        h_real = spectrum[:half] + skip
        h_imag = jnp.where(first, 0.0, spectrum[half:])
        h_last = jnp.where(first, spectrum[half:] + skip, h_real)

        def block(before, now):
            window = jnp.concatenate([before, now], 0)
            x = dot(f_high, window) + dot(f_low, window)
            a, b = x[:half], x[half:]
            y = jnp.concatenate([a * h_real - b * h_imag, a * h_imag + b * h_last], 0)
            y_high = y.astype(BF16)
            y_low = (y - y_high.astype(F32)).astype(BF16)
            return dot(i_high, y_high) + dot(i_low, y_high) + dot(i_high, y_low)

        slot = lax.rem(c, 2)
        upper = block(prod[c, 0:half, :], prod[c, half:, :])
        gath[p, c, pl.ds(half, half), :] = (query[slot, pl.ds(half, half), :] * upper).astype(BF16)
        for way in range(2):
            g_copy(p, c, way, 1).start()

        @pl.when(s > 0)
        def _():
            ph_copy(c).wait_recv()

        lower = block(phalo[c], prod[c, 0:half, :])
        gath[p, c, pl.ds(0, half), :] = (query[slot, pl.ds(0, half), :] * lower).astype(BF16)
        for way in range(2):
            g_copy(p, c, way, 0).start()

    def pass_on(c):
        for way in (1, 0):
            g_copy(beside[way], c, way, way).wait_recv()
            d_copy(beside[way], c, way).start()
        for way in (0, 1):
            g_copy(beside[way], c, way, 1 - way).wait_recv()

    tile = 1024

    def project(c, owners, last=False):
        for q in owners:
            w_copy(q, c).wait()

        @pl.loop(0, channels // tile)
        def _(n):
            lanes = pl.ds(pl.multiple_of(n * tile, tile), tile)
            total = acc[:, lanes]
            for q in owners:
                total = total + dot(gath[q, c], wbuf[q, c, :, lanes])
            if last:
                out_ref[:, lanes] = total.astype(BF16)
            else:
                acc[:, lanes] = total

    @pl.loop(0, chunks + 3)
    def _(i):
        @pl.when(i + 1 < chunks)
        def _():
            feat_copy(i + 1).wait()
            share(i + 1)

        @pl.when(i < chunks)
        def _():
            earlier(i)

        @pl.when(i + 1 < chunks)
        def _():
            later(i + 1)
            hand_on(i + 1)

        @pl.when(i < chunks)
        def _():
            gate(i)

        @pl.when((i >= 2) & (i < chunks + 2))
        def _():
            pass_on(i - 2)
            project(i - 2, (p,) + beside)

        @pl.when(i >= 3)
        def _():
            for way in range(2):
                d_copy(across, i - 3, way).wait_recv()

            @pl.when(i < chunks + 2)
            def _():
                project(i - 3, (across,))

    project(chunks - 1, (across,), last=True)

    @pl.loop(0, chunks)
    def _(c):
        @pl.when(s < seqs - 1)
        def _():
            fh_copy(c).wait_send()
            ph_copy(c).wait_send()

        for k in range(1, seqs):
            tap_copy(c, k).wait_send()
        for way in range(2):
            for part in range(2):
                g_copy(p, c, way, part).wait_send()
            d_copy(beside[way], c, way).wait_send()


def fused(seqs, tps, features, short_filter, medium_filter, skip_gain, out_weight):
    _, rows, channels = features.shape
    own_taps = medium_filter.shape[0]
    short = short_filter.shape[0]
    width = 256
    chunks = channels // width
    edge = 16
    forward, inverse = transforms(rows)
    sizes = (seqs, tps, chunks, width, rows, channels, own_taps, short)
    vmem = pl.BlockSpec(memory_space=pltpu.VMEM)
    anywhere = pl.BlockSpec(memory_space=pl.ANY)
    dma = pltpu.SemaphoreType.DMA
    columns = out_weight.shape[1]
    return pl.pallas_call(
        functools.partial(kernel, sizes),
        out_shape=jax.ShapeDtypeStruct((rows, columns), BF16),
        in_specs=[anywhere, vmem, vmem, vmem, vmem, vmem, anywhere],
        out_specs=vmem,
        scratch_shapes=[
            pltpu.VMEM((chunks, 3, rows, width), BF16),
            pltpu.VMEM((chunks, 3, edge, width), BF16),
            pltpu.VMEM((3, rows + 8, width), F32),
            pltpu.VMEM((2, rows, width), F32),
            pltpu.VMEM((chunks, rows, width), BF16),
            pltpu.VMEM((chunks, rows // 2, width), BF16),
            pltpu.VMEM((chunks, seqs * own_taps, width), BF16),
            pltpu.VMEM((tps, chunks, rows, width), BF16),
            pltpu.VMEM((tps, chunks, width, columns), BF16),
            pltpu.VMEM((rows, columns), F32),
            dma((chunks,)),
            dma((tps, chunks)),
            dma((chunks,)),
            dma((chunks,)),
            dma((chunks,)),
            dma((chunks,)),
            dma((chunks, seqs - 1)),
            dma((chunks, seqs - 1)),
            dma((chunks, 4)),
            dma((chunks, 4)),
            dma((chunks, 2)),
            dma((chunks, 2)),
        ],
        compiler_params=pltpu.CompilerParams(
            collective_id=0, has_side_effects=True, vmem_limit_bytes=56 * 1024 * 1024
        ),
    )(
        features,
        short_filter.transpose(1, 0, 2),
        medium_filter,
        skip_gain.reshape(1, channels),
        jnp.asarray(forward),
        jnp.asarray(inverse),
        out_weight,
    )


def solution(mesh):
    in_specs = (P(None, "seq", "tp"), P(None, None, "tp"), P("seq", "tp"), P("tp"), P(None, "tp"))
    out_specs = P("seq", "tp")
    seqs, tps = mesh.shape["seq"], mesh.shape["tp"]

    def body(features, short_filter, medium_filter, skip_gain, out_weight):
        taps_all = seqs * medium_filter.shape[0]
        fits = (
            tps == 4
            and seqs > 1
            and medium_filter.shape[0] % 16 == 0
            and features.shape[1] == 2 * taps_all
            and features.shape[2] % 1024 == 0
            and short_filter.shape[0] <= 9
        )
        if fits:
            return fused(
                seqs, tps, features, short_filter, medium_filter, skip_gain, out_weight
            )
        return on_device(features, short_filter, medium_filter, skip_gain, out_weight)

    return jax.shard_map(body, mesh=mesh, in_specs=in_specs, out_specs=out_specs, check_vma=False)
```
